256 devices in a mesh: row: 2 (over core), col: 4 (over x), depth: 32 (over z, y).
Axes of the slice: x: 4, y: 4, z: 8, core: 2. Of those that a mesh axis runs over, the one named last changes fastest.
Arguments:
- parent_block: float32 [32, 512, 512], P('depth', 'row', 'col')
- parent_right: float32 [32, 512, 3072], P('depth', 'row', 'col'), may hold values from -5 to 5
- parent_below: float32 [32, 3072, 512], P('depth', 'row', 'col'), may hold values from -5 to 5
- grand_block: float32 [32, 3072, 3072], P('depth', 'row', 'col'), may hold values from -6 to 6
- lower_parent: bfloat16 [32, 512, 512], P('depth', 'row', 'col'), may hold values from -0.75 to 0.75
- lower_grand: bfloat16 [32, 3072, 512], P('depth', 'row', 'col'), may hold values from -2 to 2
- upper_parent: bfloat16 [32, 512, 512], P('depth', 'row', 'col'), may hold values from -0.75 to 0.75
- upper_grand: bfloat16 [32, 512, 3072], P('depth', 'row', 'col'), may hold values from -2 to 2
- lower_inverse: bfloat16 [32, 512, 512], P('depth'), may hold values from -0.25 to 0.25
- upper_inverse: bfloat16 [32, 512, 512], P('depth'), may hold values from -0.25 to 0.25
- pivot_order: int32 [32, 512], P('depth'), may hold values from 0 to 511, each once within a row
- live_width: int32 [32], P('depth'), may hold values from 128 to 512, as said below
- tile_pattern: int32 [32, 24], P('depth'), may hold values 0 or 1
Outputs:
- grand_schur: float32 [32, 3072, 3072], P('depth', 'row', 'col')
The draws below stay inside these ranges and needn't reach their ends.
Inputs may be any that keep to these rules, and one draw needn't show every extreme that they name: `live_width`: some layer has all 512 columns live and another only 128.
All inputs are finite; a program needn't handle non-finite values. No bound on the sum of `tile_pattern` on one device may be relied on, other than what follows from the above.
Results may differ from the reference program's by a relative error of at most 0.002.
Values may be sent and summed in bfloat16 or wider, within the bound.
No kernel may reach another device: no remote copies, remote signals or barrier semaphores. Data moves between devices by JAX's collectives and lax.ppermute only.
A program may use at most 64 MiB of HBM per device.

```python
import jax
import jax.numpy as jnp
from jax import lax

W = 512
P_SIZE = 512
G = 3072
TILE = 128
NEWTON = 3
N_DEPTH = 32


def draw_parent_block(key, part):
    key = jax.random.fold_in(key, 11)
    first_key, second_key = jax.random.split(key)
    spread = P_SIZE ** (-0.5)
    noise = 1.7 * spread * jax.random.normal(first_key, (N_DEPTH, P_SIZE, P_SIZE), jnp.float32)
    diagonal = jax.random.uniform(second_key, (N_DEPTH, P_SIZE), jnp.float32, 3.0, 5.0)
    return noise + diagonal[:, :, None] * jnp.eye(P_SIZE, dtype=jnp.float32)[None, :, :]


def draw_live_width(key, part):
    key = jax.random.fold_in(key, 5)
    first_key, second_key, third_key = jax.random.split(key, 3)
    widths = jax.random.randint(first_key, (N_DEPTH,), W // 4, W + 1, dtype=jnp.int32)
    widest = jax.random.randint(second_key, (), 0, N_DEPTH, dtype=jnp.int32)
    narrow = (widest + jax.random.randint(third_key, (), 1, N_DEPTH, dtype=jnp.int32)) % N_DEPTH
    widths = widths.at[widest].set(W)
    return widths.at[narrow].set(W // 4)


def touch_ends(array, own_key, smallest, high):
    extent = array.shape
    index_at = [jax.random.randint(jax.random.fold_in(own_key, axis), (), 0, extent[axis]) for axis in range(len(extent))]
    array = array.at[tuple(index_at)].set(smallest)
    longest = extent.index(max(extent))
    index_at[longest] = (index_at[longest] + 1) % extent[longest]
    return array.at[tuple(index_at)].set(high)


def block_scale(rng, dims, pieces, low, top_value):
    def one(axis_at, blocks):
        heights = jax.random.uniform(jax.random.fold_in(jax.random.fold_in(rng, 6), axis_at), (blocks,), jnp.float32, low / len(pieces), top_value / len(pieces))
        return jnp.repeat(jnp.exp(heights), dims[axis_at] // blocks).reshape((-1,) + (1,) * (len(dims) - axis_at - 1))

    factor_of = one(*pieces[0])
    for cut in pieces[1:]:
        factor_of = factor_of * one(*cut)
    return factor_of


def scatter_about(key, shape, scale, limit, cuts=(), kind=jnp.bfloat16):
    drawn = jax.random.normal(key, shape, jnp.float32) * scale
    if len(cuts) > 0:
        drawn = block_scale(key, shape, cuts, -0.22, 0.18) * drawn
    return jnp.clip(drawn, min=-limit, max=limit).astype(kind)


def setup_inputs(seed: int = 0) -> dict:
    seeds = jax.random.split(jax.random.key(seed), 14)
    parent_block = draw_parent_block(jax.random.fold_in(seeds[13], 71), 0)
    parent_right = scatter_about(seeds[1], (N_DEPTH, P_SIZE, G), 0.35, 5.0, ((0, 32), (1, 2), (2, 4)), jnp.float32)
    parent_below = scatter_about(seeds[2], (N_DEPTH, G, P_SIZE), 0.35, 5.0, ((0, 32), (1, 2), (2, 4)), jnp.float32)
    grand_block = scatter_about(seeds[3], (N_DEPTH, G, G), 1.0, 6.0, ((0, 32), (1, 2), (2, 4)), jnp.float32)
    lower_parent = scatter_about(seeds[4], (N_DEPTH, P_SIZE, W), 0.05, 0.75, ((0, 32), (1, 2), (2, 4)))
    lower_grand = scatter_about(seeds[5], (N_DEPTH, G, W), 0.15, 2.0, ((0, 32), (1, 2), (2, 4)))
    upper_parent = scatter_about(seeds[6], (N_DEPTH, W, P_SIZE), 0.05, 0.75, ((0, 32), (1, 2), (2, 4)))
    upper_grand = scatter_about(seeds[7], (N_DEPTH, W, G), 0.15, 2.0, ((0, 32), (1, 2), (2, 4)))
    lower_inverse = scatter_about(seeds[8], (N_DEPTH, W, W), W ** -0.5, 0.25, ((0, 32),))
    upper_inverse = scatter_about(seeds[9], (N_DEPTH, W, W), W ** -0.5, 0.25, ((0, 32),))
    pivot_order = jax.vmap(lambda own: jax.random.permutation(own, W))(jax.random.split(seeds[10], N_DEPTH)).reshape((N_DEPTH, W)).astype(jnp.int32)
    live_width = draw_live_width(jax.random.fold_in(seeds[13], 71), 0)
    tile_pattern = touch_ends((jax.random.randint(seeds[12], (N_DEPTH, G // TILE), 0, 4) < 3).astype(jnp.int32), jax.random.fold_in(seeds[12], 1), 0, 1)
    return dict(parent_block=parent_block, parent_right=parent_right, parent_below=parent_below, grand_block=grand_block, lower_parent=lower_parent, lower_grand=lower_grand, upper_parent=upper_parent, upper_grand=upper_grand, lower_inverse=lower_inverse, upper_inverse=upper_inverse, pivot_order=pivot_order, live_width=live_width, tile_pattern=tile_pattern)


def newton_inverse(matrix):
    inverse = jnp.eye(P_SIZE, dtype=matrix.dtype) / jnp.diagonal(matrix)[None, :]
    for step in range(NEWTON):
        product = jnp.dot(matrix, inverse, precision=lax.Precision.HIGHEST)
        inverse = 2.0 * inverse - jnp.dot(inverse, product, precision=lax.Precision.HIGHEST)
    return inverse


def leaf_update(operands):
    (parent_block, parent_right, parent_below, grand_block, lower_parent, lower_grand,
     upper_parent, upper_grand, lower_inverse, upper_inverse, pivot_order, live_width, tile_pattern) = operands
    live = (jnp.arange(W, dtype=jnp.int32) < live_width).astype(jnp.float32)
    tile_live = jnp.repeat(tile_pattern, TILE).astype(jnp.float32)
    panel_parent = (jnp.dot(lower_parent, upper_inverse, preferred_element_type=jnp.float32) * live[None, :]).astype(jnp.bfloat16)
    panel_grand = (jnp.dot(lower_grand, upper_inverse, preferred_element_type=jnp.float32) * live[None, :] * tile_live[:, None]).astype(jnp.bfloat16)
    upper_pivot = (jnp.dot(lower_inverse, upper_parent[pivot_order], preferred_element_type=jnp.float32) * live[:, None]).astype(jnp.bfloat16)
    upper_far = (jnp.dot(lower_inverse, upper_grand[pivot_order], preferred_element_type=jnp.float32) * live[:, None] * tile_live[None, :]).astype(jnp.bfloat16)
    part_pivot = parent_block - jnp.dot(panel_parent, upper_pivot, preferred_element_type=jnp.float32)
    part_right = parent_right - jnp.dot(panel_parent, upper_far, preferred_element_type=jnp.float32)
    part_below = parent_below - jnp.dot(panel_grand, upper_pivot, preferred_element_type=jnp.float32)
    part_corner = grand_block - jnp.dot(panel_grand, upper_far, preferred_element_type=jnp.float32)
    return (part_pivot, part_right, part_below, part_corner)


def level_one(operands):
    pair_pivot, pair_right, pair_below, pair_corner = operands
    inverse_b = newton_inverse(pair_pivot).astype(jnp.bfloat16)
    level_lower = jnp.dot(pair_below.astype(jnp.bfloat16), inverse_b, preferred_element_type=jnp.float32).astype(jnp.bfloat16)
    return pair_corner - jnp.dot(level_lower, pair_right.astype(jnp.bfloat16), preferred_element_type=jnp.float32)


def reference(parent_block, parent_right, parent_below, grand_block, lower_parent, lower_grand,
              upper_parent, upper_grand, lower_inverse, upper_inverse, pivot_order, live_width, tile_pattern):
    parts = lax.map(leaf_update, (parent_block, parent_right, parent_below, grand_block, lower_parent, lower_grand,
                                  upper_parent, upper_grand, lower_inverse, upper_inverse, pivot_order, live_width, tile_pattern))
    pairs = tuple(block[0::2] + block[1::2] for block in parts)
    levels = lax.map(level_one, pairs)
    quads = levels[0::2] + levels[1::2]
    return jnp.repeat(quads, 4, axis=0)
```

```python
import jax
import jax.numpy as jnp
from jax import lax
from jax.sharding import PartitionSpec as P

W = 512
P_SIZE = 512
TILE = 128
NEWTON = 3
PART_A = 512
F16_TOP = 32768.0


def swapped(block, axis, mask):
    route = [(low, low ^ mask) for low in range(lax.axis_size(axis))]
    return lax.ppermute(block, axis, route)


def ring_gather(block, axis):
    middle = block.shape[0] // 2
    near = swapped(block, axis, 1)
    far = swapped(block, axis, 3)
    first = swapped(near[:middle], axis, 3)
    second = swapped(far[middle:], axis, 1)
    return near, far, jnp.concatenate([first, second], axis=0)


def in_ring_order(matrix, index, size):
    return jnp.concatenate(
        [
            lax.dynamic_slice_in_dim(matrix, (index ^ mask) * size, size, axis=0)
            for mask in (0, 1, 3, 2)
        ],
        axis=0,
    )


def in_order(flag, own, other):
    return jnp.concatenate(
        [jnp.where(flag == 0, own, other), jnp.where(flag == 0, other, own)], axis=0
    )


def newton_inverse(matrix):
    where = lax.broadcasted_iota(jnp.int32, matrix.shape, 0) == lax.broadcasted_iota(
        jnp.int32, matrix.shape, 1
    )
    only = jnp.where(where, matrix, 0.0)
    by_row = 1.0 / jnp.sum(only, axis=1)
    by_col = 1.0 / jnp.sum(only, axis=0)
    inverse = jnp.where(where, 2.0 * by_col[None, :], 0.0) - by_row[:, None] * (
        matrix * by_col[None, :]
    )
    for step in range(NEWTON - 1):
        product = jnp.dot(matrix, inverse, precision=lax.Precision.HIGHEST)
        inverse = 2.0 * inverse - jnp.dot(inverse, product, precision=lax.Precision.HIGHEST)
    return inverse


def dot(left, right):
    return jnp.dot(left, right, preferred_element_type=jnp.float32)


def body(
    parent_block,
    parent_right,
    parent_below,
    grand_block,
    lower_parent,
    lower_grand,
    upper_parent,
    upper_grand,
    lower_inverse,
    upper_inverse,
    pivot_order,
    live_width,
    tile_pattern,
):
    row_index = lax.axis_index("row")
    col_index = lax.axis_index("col")
    depth_index = lax.axis_index("depth")
    row_count = lax.axis_size("row")
    col_count = lax.axis_size("col")
    h = (depth_index >> 1) & 1
    g = (depth_index ^ (depth_index >> 1)) & 1
    tile_count = tile_pattern.shape[1]
    row_tiles = tile_count // row_count
    col_tiles = tile_count // col_count
    live = jnp.arange(W, dtype=jnp.int32) < live_width[0]
    row_live = jnp.repeat(
        lax.dynamic_slice_in_dim(tile_pattern[0], row_index * row_tiles, row_tiles), TILE
    ).astype(jnp.float32)
    col_live = jnp.repeat(
        lax.dynamic_slice_in_dim(tile_pattern[0], col_index * col_tiles, col_tiles), TILE
    ).astype(jnp.float32)
    bf16 = jnp.bfloat16
    width = lower_grand.shape[2]

    parent_near = swapped(lower_parent[0], "col", 1)
    parent_far = swapped(lower_parent[0], "col", 3)
    parent_across = swapped(lower_parent[0], "col", 2)
    grand_blocks = ring_gather(lower_grand[0], "col")
    full_parent = lax.all_gather(upper_parent[0], "row", axis=0, tiled=True)
    full_grand = lax.all_gather(upper_grand[0], "row", axis=0, tiled=True)
    top = jnp.max(jnp.abs(grand_block[0]))

    solve_right = in_ring_order(
        jnp.where(live[None, :], upper_inverse[0], jnp.zeros((), bf16)), col_index, width
    )
    chosen = (pivot_order[0][:, None] == jnp.arange(W, dtype=jnp.int32)[None, :]).astype(bf16)
    solve_left = dot(
        jnp.where(live[:, None], lower_inverse[0], jnp.zeros((), bf16)), chosen
    ).astype(bf16)

    upper_pivot = dot(solve_left, full_parent).astype(bf16)
    upper_far = (dot(solve_left, full_grand) * col_live[None, :]).astype(bf16)
    panel_parent = dot(
        jnp.concatenate([lower_parent[0], parent_near, parent_far, parent_across], axis=1),
        solve_right,
    ).astype(bf16)

    pivot_sum = parent_block[0] - dot(panel_parent, upper_pivot)
    pivot_mine = pivot_sum + swapped(pivot_sum, "depth", 1)
    pivot_other = swapped(pivot_mine, "depth", 3)

    def halves(block, flag, rows, start=0):
        keep = lax.dynamic_slice_in_dim(block, start + flag * rows, rows, axis=0)
        give = lax.dynamic_slice_in_dim(block, start + (1 - flag) * rows, rows, axis=0)
        return keep, give

    def pair_halves(block):
        keep, give = halves(block, g, block.shape[0] // 2)
        own = (keep + swapped(give, "depth", 1)).astype(bf16)
        sibling = swapped(own, "depth", 1)
        mine = in_order(g, own, sibling)
        other = in_order(g, swapped(own, "depth", 3), swapped(sibling, "depth", 3))
        return mine, other

    right_mine, right_other = pair_halves(parent_right[0] - dot(panel_parent, upper_far))
    right_full = lax.all_gather(
        jnp.stack([right_mine, right_other]), "row", axis=1, tiled=True
    )

    panel_grand = (
        dot(jnp.concatenate([lower_grand[0], *grand_blocks], axis=1), solve_right)
        * row_live[:, None]
    ).astype(bf16)
    below_mine, below_other = pair_halves(parent_below[0] - dot(panel_grand, upper_pivot))

    bound = top + jnp.sum(
        jnp.max(jnp.abs(panel_grand), axis=0).astype(jnp.float32)
        * jnp.max(jnp.abs(upper_far), axis=1).astype(jnp.float32)
    )
    bound = jnp.full((8, 128), bound, jnp.float32)
    bound = bound + swapped(bound, "depth", 1)
    bound = bound + swapped(bound, "depth", 3)
    bound = jnp.maximum(bound[0, 0], 1e-30)
    into = F16_TOP / bound
    back = bound * (1.0 / F16_TOP)

    def code(block):
        return (block * into).astype(jnp.float16)

    def decode(block):
        return block.astype(jnp.float32) * back

    def corner(start, rows):
        return lax.dynamic_slice_in_dim(grand_block[0], start, rows, axis=0) - dot(
            lax.dynamic_slice_in_dim(panel_grand, start, rows, axis=0), upper_far
        )

    def quad_sum(start, rows, flag_one, mask_one, flag_two, mask_two):
        half, quarter = rows // 2, rows // 4
        at = start + flag_one * half
        away = start + (1 - flag_one) * half
        arrived = swapped(code(corner(away, half)), "depth", mask_one)
        kept = corner(at, half) + decode(arrived)
        keep, give = halves(kept, flag_two, quarter)
        own = keep + decode(swapped(code(give), "depth", mask_two))
        coded = code(own)
        beside = swapped(coded, "depth", mask_two)
        here, there = flag_two * quarter, (1 - flag_two) * quarter
        return [
            (at + here, own),
            (at + there, decode(beside)),
            (away + here, decode(swapped(coded, "depth", mask_one))),
            (away + there, decode(swapped(beside, "depth", mask_one))),
        ]

    rows_all = grand_block.shape[1]
    pieces = quad_sum(0, PART_A, g, 1, h, 3)
    pieces += quad_sum(PART_A, rows_all - PART_A, h, 3, g, 1)

    first = row_index == 0
    traded = swapped(jnp.where(first, pivot_other, pivot_mine), "row", 1)
    kept = jnp.where(first, pivot_mine, pivot_other)
    pivot_rows = in_order(row_index, kept, traded)
    near, far, across = ring_gather(pivot_rows, "col")
    blocks = [pivot_rows, near, far, across]
    places = [col_index ^ mask for mask in (0, 1, 3, 2)]
    pivot_whole = jnp.concatenate(
        [
            sum(jnp.where(place == k, block, 0.0) for place, block in zip(places, blocks))
            for k in range(col_count)
        ],
        axis=1,
    )
    inverse_one = newton_inverse(pivot_whole).astype(bf16)
    inverse_two = swapped(inverse_one, "row", 1)
    inverse_mine = in_ring_order(jnp.where(first, inverse_one, inverse_two), col_index, width)
    inverse_other = in_ring_order(jnp.where(first, inverse_two, inverse_one), col_index, width)

    def level_lower(block, inverse):
        whole = jnp.concatenate([block, *ring_gather(block, "col")], axis=1)
        return dot(whole, inverse).astype(bf16)

    lower_mine = level_lower(below_mine, inverse_mine)
    lower_other = level_lower(below_other, inverse_other)
    result = -(dot(lower_mine, right_full[0]) + dot(lower_other, right_full[1]))
    for start, piece in pieces:
        part = lax.dynamic_slice_in_dim(result, start, piece.shape[0], axis=0)
        result = lax.dynamic_update_slice_in_dim(result, part + piece, start, axis=0)
    return result[None]


def solution(mesh):
    return jax.shard_map(
        body,
        mesh=mesh,
        in_specs=(
            P("depth", "row", "col"),
            P("depth", "row", "col"),
            P("depth", "row", "col"),
            P("depth", "row", "col"),
            P("depth", "row", "col"),
            P("depth", "row", "col"),
            P("depth", "row", "col"),
            P("depth", "row", "col"),
            P("depth", None, None),
            P("depth", None, None),
            P("depth", None),
            P("depth"),
            P("depth", None),
        ),
        out_specs=P("depth", "row", "col"),
        check_vma=False,
    )
```

```python
import jax
import jax.numpy as jnp
from jax import lax
from jax.experimental import pallas as pl
from jax.experimental.pallas import tpu as pltpu
from jax.sharding import PartitionSpec as P

TILE = 128
NEWTON = 3
COLUMNS = 256
RING = (0, 1, 3, 2)
F32 = jnp.float32
BF16 = jnp.bfloat16
I16 = jnp.int16
SCALARS = pl.BlockSpec(memory_space=pltpu.SMEM)


def swapped(block, axis, mask):
    route = [(low, low ^ mask) for low in range(lax.axis_size(axis))]
    return lax.ppermute(block, axis, route)


def ring_gather(block, axis):
    return [swapped(block, axis, mask) for mask in RING[1:]]


def dot(left, right):
    return jnp.dot(left, right, preferred_element_type=F32)


def call(kernel, outs, args, specs=None, grid=None, out_specs=None, scratch=(), flops=0, aliases=None):
    size = sum(a.size * a.dtype.itemsize for a in list(args) + list(outs))
    more = {}
    if grid is not None:
        more = dict(grid=grid, out_specs=out_specs)
    if specs is not None:
        more["in_specs"] = specs
    if aliases is not None:
        more["input_output_aliases"] = aliases
    return pl.pallas_call(
        kernel,
        out_shape=list(outs),
        scratch_shapes=list(scratch),
        compiler_params=pltpu.CompilerParams(vmem_limit_bytes=40 * 2**20),
        cost_estimate=pl.CostEstimate(flops=flops, bytes_accessed=size, transcendentals=0),
        **more,
    )(*args)


def shape(dims, dtype):
    return jax.ShapeDtypeStruct(dims, dtype)


def start_at(block, size):
    return pl.ds(pl.multiple_of(block * size, size), size)


def iota(dims, axis):
    return lax.broadcasted_iota(jnp.int32, dims, axis)


def encode(block, coded_ref):
    rows = block.shape[0]
    most = jnp.maximum(jnp.max(jnp.abs(block), axis=0, keepdims=True), 1e-30)
    power = jnp.ceil(jnp.log2(most) + 0.01)
    scale = 0.98 * jnp.exp2(15.0 - power)
    coded_ref[:rows, :] = jnp.round(block * scale).astype(jnp.int32).astype(I16)
    coded_ref[rows:, :] = jnp.broadcast_to(power, (16, block.shape[1])).astype(jnp.int32).astype(I16)


def decode(coded_ref):
    rows = coded_ref.shape[0] - 16
    power = coded_ref[rows:, :].astype(jnp.int32).astype(F32)[:1, :]
    scale = jnp.exp2(power - 15.0) * (1.0 / 0.98)
    return coded_ref[:rows, :].astype(jnp.int32).astype(F32) * scale


def leaf_parent_kernel(
    at, live, tiles, order, upper_inverse, lower_inverse, pivot_own, pivot_across, far_own, far_across,
    lower_0, lower_1, lower_3, lower_2, parent_block, parent_right,
    solve_right, strip, give, keep, solve_left, right,
):
    row, col, g = at[0], at[1], at[2]
    width = lower_0.shape[1]
    size = upper_inverse.shape[0]
    half_k = far_own.shape[0]
    wide = far_own.shape[1]
    shown = iota((width, size), 1) < live[0]
    for k, mask in enumerate(RING):
        block = upper_inverse[start_at(col ^ mask, width), :].astype(F32)
        solve_right[k * width : (k + 1) * width, :] = jnp.where(shown, block, 0.0).astype(BF16)
    chosen = jnp.where(iota((size, size), 0) == order[...], 1.0, 0.0).astype(BF16)
    masked = jnp.where(iota((size, size), 0) < live[0], lower_inverse[...].astype(F32), 0.0).astype(BF16)
    solve_left[...] = lax.dot_general(
        masked, chosen, (((1,), (1,)), ((), ())), preferred_element_type=F32
    ).astype(BF16)
    left_own = solve_left[:, start_at(row, half_k)]
    left_across = solve_left[:, start_at(1 - row, half_k)]
    count = wide // TILE
    far = dot(left_own, far_own[...]) + dot(left_across, far_across[...])
    for t in range(count):
        flag = tiles[0, col * count + t].astype(F32)
        strip[:, t * TILE : (t + 1) * TILE] = (far[:, t * TILE : (t + 1) * TILE] * flag).astype(BF16)
    strip[:, wide:] = (dot(left_own, pivot_own[...]) + dot(left_across, pivot_across[...])).astype(BF16)
    lower = jnp.concatenate([lower_0[...], lower_1[...], lower_3[...], lower_2[...]], axis=1)
    panel = dot(lower, solve_right[...]).astype(BF16)
    right[...] = parent_right[...] - dot(panel, strip[:, :wide])
    pivot = parent_block[...] - dot(panel, strip[:, wide:])
    rows = right.shape[0] // 2
    give[:, :wide] = right[start_at(1 - g, rows), :]
    keep[:, :wide] = right[start_at(g, rows), :]
    for ref in (give, keep):
        ref[:, wide : wide + width] = pivot[:rows, :]
        ref[:, wide + width :] = pivot[rows:, :]


def parent_pair_kernel(keep, came, pivot, right):
    rows, wide = right.shape
    total = keep[...] + came[...]
    right[...] = total[:, :wide].astype(BF16)
    pivot[:rows, :] = total[:, wide : wide + TILE]
    pivot[rows:, :] = total[:, wide + TILE :]


def leaf_grand_kernel(part, at, tiles, lower_0, lower_1, lower_3, lower_2, solve_right, strip, parent_below, grand, *rest):
    if part == 0:
        corner, coded, below, panel = rest
    else:
        before, corner, coded, give, keep, panel = rest
    row, g = at[0], at[2]
    j = pl.program_id(0)
    wide = strip.shape[1] - TILE

    @pl.when(j == 0)
    def _():
        lower = jnp.concatenate([lower_0[...], lower_1[...], lower_3[...], lower_2[...]], axis=1)
        whole = dot(lower, solve_right[...])
        count = whole.shape[0] // TILE
        for t in range(count):
            flag = tiles[0, (row * 2 + part) * count + t].astype(F32)
            panel[t * TILE : (t + 1) * TILE, :] = (whole[t * TILE : (t + 1) * TILE, :] * flag).astype(BF16)
        found = parent_below[...] - dot(panel[...], strip[:, wide:])
        if part == 0:
            below[...] = found
        else:
            give[...] = jnp.where(g == 0, found, before[...])
            keep[...] = jnp.where(g == 0, before[...], found)

    block = grand[...] - dot(panel[...], strip[:, pl.ds(pl.multiple_of(j * COLUMNS, COLUMNS), COLUMNS)])
    corner[...] = block
    encode(block, coded)


def corner_pair_kernel(corner, came, total, coded):
    block = corner[...] + decode(came)
    total[...] = block
    encode(block, coded)


def newton_kernel(at, block_0, block_1, block_3, block_2, out, matrix, inverse):
    col = at[1]
    size = matrix.shape[0]
    for mask, block in zip(RING, (block_0, block_1, block_3, block_2)):
        matrix[:, start_at(col ^ mask, block.shape[1])] = block[...]
    where = iota((size, size), 0) == iota((size, size), 1)
    only = jnp.where(where, matrix[...], 0.0)
    by_row = 1.0 / jnp.sum(only, axis=1, keepdims=True)
    by_col = 1.0 / jnp.sum(only, axis=0, keepdims=True)
    inverse[...] = jnp.where(where, 2.0 * by_col, 0.0) - by_row * (matrix[...] * by_col)
    for step in range(NEWTON - 1):
        held = inverse[...]
        product = jnp.dot(matrix[...], held, precision=lax.Precision.HIGHEST, preferred_element_type=F32)
        inverse[...] = 2.0 * held - jnp.dot(held, product, precision=lax.Precision.HIGHEST, preferred_element_type=F32)
    out[...] = inverse[...].astype(BF16)


def level_lower_kernel(which, at, block_0, block_1, block_3, block_2, inverse_own, inverse_came, out, inverse):
    row, col = at[0], at[1]

    @pl.when(pl.program_id(0) == 0)
    def _():
        for k, mask in enumerate(RING):
            here = slice(k * TILE, (k + 1) * TILE)

            @pl.when(row == which)
            def _():
                inverse[here, :] = inverse_own[start_at(col ^ mask, TILE), :]

            @pl.when(row != which)
            def _():
                inverse[here, :] = inverse_came[start_at(col ^ mask, TILE), :]

    whole = jnp.concatenate([block_0[...], block_1[...], block_3[...], block_2[...]], axis=1)
    out[...] = dot(whole, inverse[...]).astype(BF16)


def right_kernel(at, own, across, out):
    row, g = at[0], at[2]
    rows = own.shape[0] // 4
    for ref, core in ((own, row), (across, 1 - row)):
        for k in range(4):
            half = g if k % 2 == 0 else 1 - g
            out[start_at((k // 2) * 4 + core * 2 + half, rows), :] = ref[k * rows : (k + 1) * rows, :]


def final_kernel(at, total, came, lower_mine, lower_other, right, *rest):
    out = rest[-1]
    size = lower_mine.shape[1]
    update = dot(lower_mine[...], right[:size, :]) + dot(lower_other[...], right[size:, :])
    out[...] = total[...] + decode(came) - update


def body(
    parent_block,
    parent_right,
    parent_below,
    grand_block,
    lower_parent,
    lower_grand,
    upper_parent,
    upper_grand,
    lower_inverse,
    upper_inverse,
    pivot_order,
    live_width,
    tile_pattern,
):
    row_index = lax.axis_index("row")
    col_index = lax.axis_index("col")
    depth_index = lax.axis_index("depth")
    h = (depth_index >> 1) & 1
    g = (depth_index ^ (depth_index >> 1)) & 1
    at = jnp.stack([row_index, col_index, g, h])
    size = upper_inverse.shape[2]
    rows, wide = grand_block.shape[1:]
    width = lower_grand.shape[2]
    part_rows = rows // 2
    strips = wide // COLUMNS

    parents = ring_gather(lower_parent[0], "col")
    across_pivot = swapped(upper_parent[0], "row", 1)
    across_far = swapped(upper_grand[0], "row", 1)
    grands = ring_gather(lower_grand[0], "col")
    solve_right, strip, give, keep = call(
        leaf_parent_kernel,
        [
            shape((size, size), BF16),
            shape((size, wide + width), BF16),
            shape((parent_right.shape[1] // 2, wide + 2 * width), F32),
            shape((parent_right.shape[1] // 2, wide + 2 * width), F32),
        ],
        [
            at, live_width, tile_pattern, pivot_order, upper_inverse[0], lower_inverse[0],
            upper_parent[0], across_pivot, upper_grand[0], across_far,
            lower_parent[0], *parents, parent_block[0], parent_right[0],
        ],
        specs=[SCALARS] * 3 + [pl.BlockSpec(memory_space=pltpu.VMEM)] * 13,
        scratch=[pltpu.VMEM((size, size), BF16), pltpu.VMEM(parent_right.shape[1:], F32)],
        flops=2 * size * size * (size + wide + width),
    )

    came = swapped(give, "depth", 1)
    pivot_mine, right_own = call(
        parent_pair_kernel,
        [shape(parent_block.shape[1:], F32), shape((parent_right.shape[1] // 2, wide), BF16)],
        [keep, came],
    )
    pivot_other = swapped(pivot_mine, "depth", 3)
    right_sibling = swapped(right_own, "depth", 1)
    right_pair = jnp.concatenate([right_own, right_sibling], axis=0)
    right_four = jnp.concatenate([right_pair, swapped(right_pair, "depth", 3)], axis=0)

    def leaf_grand(part, before):
        outs = [shape((part_rows, wide), F32), shape((part_rows + 16, wide), I16)]
        below_spec = pl.BlockSpec((part_rows, width), lambda j: (0, 0))
        here_spec = pl.BlockSpec((part_rows, width), lambda j: (part, 0))
        out_specs = [
            pl.BlockSpec((part_rows, COLUMNS), lambda j: (0, j)),
            pl.BlockSpec((part_rows + 16, COLUMNS), lambda j: (0, j)),
        ]
        count = 1 if part == 0 else 2
        return call(
            lambda *refs: leaf_grand_kernel(part, *refs),
            outs + [shape((part_rows, width), F32)] * count,
            [at, tile_pattern, lower_grand[0], *grands, solve_right, strip, parent_below[0], grand_block[0], *before],
            specs=[SCALARS] * 2
            + [here_spec] * 4
            + [
                pl.BlockSpec((size, size), lambda j: (0, 0)),
                pl.BlockSpec((size, wide + width), lambda j: (0, 0)),
                here_spec,
                pl.BlockSpec((part_rows, COLUMNS), lambda j: (part, j)),
            ]
            + [below_spec] * len(before),
            grid=(strips,),
            out_specs=out_specs + [below_spec] * count,
            scratch=[pltpu.VMEM((part_rows, size), BF16)],
            flops=2 * part_rows * size * (size + wide + width),
        )

    corner_0, coded_0, below_0 = leaf_grand(0, [])
    corner_1, coded_1, below_give, below_keep = leaf_grand(1, [below_0])

    def corner_pair(corner, coded):
        return call(
            corner_pair_kernel,
            [shape((part_rows, wide), F32), shape((part_rows + 16, wide), I16)],
            [corner, coded],
            specs=[
                pl.BlockSpec((part_rows, COLUMNS), lambda j: (0, j)),
                pl.BlockSpec((part_rows + 16, COLUMNS), lambda j: (0, j)),
            ],
            grid=(strips,),
            out_specs=[
                pl.BlockSpec((part_rows, COLUMNS), lambda j: (0, j)),
                pl.BlockSpec((part_rows + 16, COLUMNS), lambda j: (0, j)),
            ],
        )

    came_0 = swapped(coded_0, "depth", 3)
    below_came = swapped(below_give, "depth", 1)
    came_1 = swapped(coded_1, "depth", 1)
    below_own = (below_keep + below_came).astype(BF16)
    below_mine = jnp.concatenate([below_own, swapped(below_own, "depth", 1)], axis=0)
    below_other = swapped(below_mine, "depth", 3)
    pair_0, coded_0 = corner_pair(corner_0, came_0)
    pair_1, coded_1 = corner_pair(corner_1, came_1)
    came_0 = swapped(coded_0, "depth", 1)
    came_1 = swapped(coded_1, "depth", 3)

    first = row_index == 0
    traded = swapped(jnp.where(first, pivot_other, pivot_mine), "row", 1)
    kept = jnp.where(first, pivot_mine, pivot_other)
    pivot_rows = jnp.concatenate(
        [jnp.where(first, kept, traded), jnp.where(first, traded, kept)], axis=0
    )
    (inverse_own,) = call(
        newton_kernel,
        [shape((size, size), BF16)],
        [at, pivot_rows, *ring_gather(pivot_rows, "col")],
        specs=[SCALARS] + [pl.BlockSpec(memory_space=pltpu.VMEM)] * 4,
        scratch=[pltpu.VMEM((size, size), F32), pltpu.VMEM((size, size), F32)],
        flops=2 * 24 * size**3,
    )
    inverse_came = swapped(inverse_own, "row", 1)

    def level_lower(which, block):
        spec = pl.BlockSpec((part_rows, width), lambda i: (i, 0))
        whole = pl.BlockSpec((size, size), lambda i: (0, 0))
        return call(
            lambda *refs: level_lower_kernel(which, *refs),
            [shape((rows, size), BF16)],
            [at, block, *ring_gather(block, "col"), inverse_own, inverse_came],
            specs=[SCALARS] + [spec] * 4 + [whole] * 2,
            grid=(2,),
            out_specs=[pl.BlockSpec((part_rows, size), lambda i: (i, 0))],
            scratch=[pltpu.VMEM((size, size), BF16)],
            flops=2 * rows * size * size,
        )[0]

    lower_mine = level_lower(0, below_mine)
    lower_other = level_lower(1, below_other)
    (right_all,) = call(
        right_kernel,
        [shape((2 * size, wide), BF16)],
        [at, right_four, swapped(right_four, "row", 1)],
        specs=[SCALARS] + [pl.BlockSpec(memory_space=pltpu.VMEM)] * 2,
    )

    def final(part, total, came, before):
        lower_spec = pl.BlockSpec((part_rows, size), lambda j, at: (part ^ at[2], 0))
        args = [at, total, came, lower_mine, lower_other, right_all, *before]
        return pl.pallas_call(
            final_kernel,
            out_shape=shape((rows, wide), F32),
            grid_spec=pltpu.PrefetchScalarGridSpec(
                num_scalar_prefetch=1,
                grid=(strips,),
                in_specs=[
                    pl.BlockSpec((part_rows, COLUMNS), lambda j, at: (0, j)),
                    pl.BlockSpec((part_rows + 16, COLUMNS), lambda j, at: (0, j)),
                    lower_spec,
                    lower_spec,
                    pl.BlockSpec((2 * size, COLUMNS), lambda j, at: (0, j)),
                ]
                + [pl.BlockSpec(memory_space=pl.ANY)] * len(before),
                out_specs=pl.BlockSpec((part_rows, COLUMNS), lambda j, at: (part, j)),
            ),
            input_output_aliases={6: 0} if before else {},
            compiler_params=pltpu.CompilerParams(vmem_limit_bytes=40 * 2**20),
            cost_estimate=pl.CostEstimate(
                flops=4 * part_rows * size * wide, bytes_accessed=13 * part_rows * wide, transcendentals=0
            ),
        )(*args)

    result = final(0, pair_0, came_0, [])
    result = final(1, pair_1, came_1, [result])
    return result[None]


def solution(mesh):
    return jax.shard_map(
        body,
        mesh=mesh,
        in_specs=(
            P("depth", "row", "col"),
            P("depth", "row", "col"),
            P("depth", "row", "col"),
            P("depth", "row", "col"),
            P("depth", "row", "col"),
            P("depth", "row", "col"),
            P("depth", "row", "col"),
            P("depth", "row", "col"),
            P("depth", None, None),
            P("depth", None, None),
            P("depth", None),
            P("depth"),
            P("depth", None),
        ),
        out_specs=P("depth", "row", "col"),
        check_vma=False,
    )
```

```python
import math

import jax
import jax.numpy as jnp
from jax import lax
from jax.experimental import pallas as pl
from jax.experimental.pallas import tpu as pltpu
from jax.sharding import PartitionSpec as P

TILE = 128
NEWTON = 3
COLUMNS = 256
VMEM = 32 * 2**20
RING = (0, 1, 3, 2)
F32 = jnp.float32
BF16 = jnp.bfloat16
I16 = jnp.int16
SCALARS = pl.BlockSpec(memory_space=pltpu.SMEM)


def swapped(block, axis, mask):
    route = [(low, low ^ mask) for low in range(lax.axis_size(axis))]
    return lax.ppermute(block, axis, route)


def ring_gather(block, axis):
    return [swapped(block, axis, mask) for mask in RING[1:]]


def dot(left, right):
    return jnp.dot(left, right, preferred_element_type=F32)


def in_hbm(*arrays):
    return [pltpu.with_memory_space_constraint(array, pltpu.HBM) for array in arrays]


def call(kernel, outs, args, specs=None, grid=None, out_specs=None, scratch=(), flops=0, aliases=None):
    size = sum(math.prod(a.shape) * jnp.dtype(a.dtype).itemsize for a in list(args) + list(outs))
    more = {}
    if grid is not None:
        more = dict(grid=grid, out_specs=out_specs)
    if specs is not None:
        more["in_specs"] = specs
    if aliases is not None:
        more["input_output_aliases"] = aliases
    return pl.pallas_call(
        kernel,
        out_shape=list(outs),
        scratch_shapes=list(scratch),
        compiler_params=pltpu.CompilerParams(vmem_limit_bytes=VMEM),
        cost_estimate=pl.CostEstimate(flops=flops, bytes_accessed=size, transcendentals=0),
        **more,
    )(*args)


def shape(dims, dtype):
    return jax.ShapeDtypeStruct(dims, dtype)


def start_at(block, size):
    return pl.ds(pl.multiple_of(block * size, size), size)


def iota(dims, axis):
    return lax.broadcasted_iota(jnp.int32, dims, axis)


def encode(block, coded_ref):
    rows = block.shape[0]
    most = jnp.maximum(jnp.max(jnp.abs(block), axis=0, keepdims=True), 1e-30)
    power = jnp.ceil(jnp.log2(most) + 0.01)
    scale = 0.98 * jnp.exp2(15.0 - power)
    coded_ref[:rows, :] = jnp.round(block * scale).astype(jnp.int32).astype(I16)
    coded_ref[rows:, :] = jnp.broadcast_to(power, (16, block.shape[1])).astype(jnp.int32).astype(I16)


def decode(coded_ref):
    rows = coded_ref.shape[0] - 16
    power = coded_ref[rows:, :].astype(jnp.int32).astype(F32)[:1, :]
    scale = jnp.exp2(power - 15.0) * (1.0 / 0.98)
    return coded_ref[:rows, :].astype(jnp.int32).astype(F32) * scale


def encode_twice(block, high_ref, low_ref):
    rows = block.shape[0]
    most = jnp.maximum(jnp.max(jnp.abs(block), axis=0, keepdims=True), 1e-30)
    power = jnp.ceil(jnp.log2(most) + 0.01)
    scaled = block * (0.98 * jnp.exp2(15.0 - power))
    high = jnp.round(scaled)
    high_ref[:rows, :] = high.astype(jnp.int32).astype(I16)
    low_ref[:rows, :] = jnp.round((scaled - high) * 2.0**15).astype(jnp.int32).astype(I16)
    for ref in (high_ref, low_ref):
        ref[rows:, :] = jnp.broadcast_to(power, (16, block.shape[1])).astype(jnp.int32).astype(I16)


def decode_twice(high_ref, low_ref):
    rows = high_ref.shape[0] - 16
    power = high_ref[rows:, :].astype(jnp.int32).astype(F32)[:1, :]
    scale = jnp.exp2(power - 15.0) * (1.0 / 0.98)
    high = high_ref[:rows, :].astype(jnp.int32).astype(F32)
    low = low_ref[:rows, :].astype(jnp.int32).astype(F32)
    return (high + low * 2.0**-15) * scale


def prepare_kernel(
    at, live, tiles, order, upper_inverse, lower_inverse, pivot_all, far_all, solve_right, strip, solve_left,
):
    col = at[1]
    size = upper_inverse.shape[0]
    width = size // len(RING)
    wide = far_all.shape[1]
    shown = iota((width, size), 1) < live[0]
    for k, mask in enumerate(RING):
        block = upper_inverse[start_at(col ^ mask, width), :].astype(F32)
        solve_right[k * width : (k + 1) * width, :] = jnp.where(shown, block, 0.0).astype(BF16)
    chosen = jnp.where(iota((size, size), 0) == order[...], 1.0, 0.0).astype(BF16)
    masked = jnp.where(iota((size, size), 0) < live[0], lower_inverse[...].astype(F32), 0.0).astype(BF16)
    solve_left[...] = lax.dot_general(
        masked, chosen, (((1,), (1,)), ((), ())), preferred_element_type=F32
    ).astype(BF16)
    count = wide // TILE
    far = dot(solve_left[...], far_all[...])
    for t in range(count):
        flag = tiles[0, col * count + t].astype(F32)
        strip[:, t * TILE : (t + 1) * TILE] = (far[:, t * TILE : (t + 1) * TILE] * flag).astype(BF16)
    strip[:, wide:] = dot(solve_left[...], pivot_all[...]).astype(BF16)


def leaf_panel_kernel(tile_count, at, tiles, *refs):
    blocks, (solve_right, strip, parent_block, parent_right, parent_below) = refs[:8], refs[8:13]
    panel, right, pivot, below, coded = refs[13:]
    row = at[0]
    height, wide = parent_right.shape
    rows = parent_below.shape[0]
    cut = blocks[0].shape[0]
    for part in (0, 1):
        lower = jnp.concatenate([ref[...] for ref in blocks[4 * part : 4 * part + 4]], axis=1)
        whole = dot(lower, solve_right[...])
        for t in range((rows - cut if part else cut) // TILE):
            flag = tiles[0, row * tile_count + part * (cut // TILE) + t].astype(F32)
            panel[part * cut + t * TILE : part * cut + (t + 1) * TILE, :] = (
                whole[t * TILE : (t + 1) * TILE, :] * flag
            ).astype(BF16)
    parent = whole[rows - cut :, :].astype(BF16)
    here = 0
    found = parent_right[...] - dot(parent, strip[:, :wide])
    right[...] = found
    for k in range(wide // TILE):
        encode(found[:, k * TILE : (k + 1) * TILE], coded.at[here : here + height + 16, :])
        here += height + 16
    found = parent_block[...] - dot(parent, strip[:, wide:])
    pivot[...] = found
    middle = here + height + 16
    encode_twice(found, coded.at[here:middle, :], coded.at[middle : middle + height + 16, :])
    here = middle + height + 16
    found = parent_below[...] - dot(panel[...], strip[:, wide:])
    below[...] = found
    encode(found, coded.at[here:, :])


def leaf_pair_kernel(right, pivot, below, coded, both, below_pair, pivot_pair):
    height, wide = right.shape
    rows = below.shape[0]
    here = 0
    for k in range(wide // TILE):
        came = decode(coded.at[here : here + height + 16, :])
        both[rows + k * height : rows + (k + 1) * height, :] = (
            right[:, k * TILE : (k + 1) * TILE] + came
        ).astype(BF16)
        here += height + 16
    middle = here + height + 16
    pivot_pair[...] = pivot[...] + decode_twice(coded.at[here:middle, :], coded.at[middle : middle + height + 16, :])
    here = middle + height + 16
    total = (below[...] + decode(coded.at[here:, :])).astype(BF16)
    below_pair[...] = total
    both[:rows, :] = total


def leaf_corner_kernel(panel, far, grand, corner, coded):
    block = grand[...] - dot(panel[...], far[...])
    corner[...] = block
    encode(block, coded)


def corner_pair_kernel(corner, came, total, coded):
    block = corner[...] + decode(came)
    total[...] = block
    encode(block, coded)


def newton_kernel(at, block_0, block_1, block_3, block_2, across, out, half, matrix, inverse):
    row, col = at[0], at[1]
    size = matrix.shape[0]
    height, width = block_0.shape
    for k, (mask, block) in enumerate(zip(RING, (block_0, block_1, block_3, block_2))):
        matrix[start_at(row, height), start_at(col ^ mask, width)] = block[...]
        matrix[start_at(1 - row, height), start_at(col ^ mask, width)] = across[k * height : (k + 1) * height, :]
    where = iota((size, size), 0) == iota((size, size), 1)
    only = jnp.where(where, matrix[...], 0.0)
    by_row = 1.0 / jnp.sum(only, axis=1, keepdims=True)
    by_col = 1.0 / jnp.sum(only, axis=0, keepdims=True)
    inverse[...] = jnp.where(where, 2.0 * by_col, 0.0) - by_row * (matrix[...] * by_col)
    for step in range(NEWTON - 1):
        held = inverse[...]
        product = jnp.dot(matrix[...], held, precision=lax.Precision.HIGHEST, preferred_element_type=F32)
        inverse[...] = 2.0 * held - jnp.dot(held, product, precision=lax.Precision.HIGHEST, preferred_element_type=F32)
    out[...] = inverse[...].astype(BF16)
    half[...] = inverse[start_at(row, half.shape[0]), :].astype(BF16)


def level_lower_kernel(at, block_0, block_1, block_3, block_2, inverse, out, ordered):
    col = at[1]

    @pl.when(pl.program_id(0) == 0)
    def _():
        for k, mask in enumerate(RING):
            ordered[k * TILE : (k + 1) * TILE, :] = inverse[start_at(col ^ mask, TILE), :]

    whole = jnp.concatenate([block_0[...], block_1[...], block_3[...], block_2[...]], axis=1)
    out[...] = dot(whole, ordered[...]).astype(BF16)


def right_kernel(at, mine, other, across, out):
    row = at[0]
    height = across.shape[0] // (2 * (out.shape[1] // TILE))
    for k in range(out.shape[1] // TILE):
        strip = slice(k * TILE, (k + 1) * TILE)
        own = mine.shape[0] // 2 + k * height
        out[start_at(row, height), strip] = mine[own : own + height, :]
        out[start_at(2 + row, height), strip] = other[own : own + height, :]
        own = k * height
        out[start_at(1 - row, height), strip] = across[own : own + height, :]
        own += across.shape[0] // 2
        out[start_at(3 - row, height), strip] = across[own : own + height, :]


def update_kernel(total_0, total_1, lower_mine, lower_other, right, out):
    size = lower_mine.shape[1]
    cut = total_0.shape[0]
    update = dot(lower_mine[...], right[:size, :]) + dot(lower_other[...], right[size:, :])
    out[:cut, :] = total_0[...] - update[:cut, :]
    out[cut:, :] = total_1[...] - update[cut:, :]


def final_kernel(part, came_0, came_1, out):
    cut = came_0.shape[0] - 16
    out[:cut, :] = part[:cut, :] + decode(came_0)
    out[cut:, :] = part[cut:, :] + decode(came_1)


def body(
    parent_block,
    parent_right,
    parent_below,
    grand_block,
    lower_parent,
    lower_grand,
    upper_parent,
    upper_grand,
    lower_inverse,
    upper_inverse,
    pivot_order,
    live_width,
    tile_pattern,
):
    row_index = lax.axis_index("row")
    col_index = lax.axis_index("col")
    at = jnp.stack([row_index, col_index])
    size = upper_inverse.shape[2]
    rows, wide = grand_block.shape[1:]
    width = lower_grand.shape[2]
    strips = wide // COLUMNS

    height = parent_right.shape[1]
    cut = (rows + height) // 2
    halves = [lower_grand[0][:cut], jnp.concatenate([lower_grand[0][cut:], lower_parent[0]], axis=0)]
    steps = [swapped(half, "col", mask) for half in halves for mask in (1, 3)]
    blocks = [halves[0], steps[0], steps[1], swapped(steps[0], "col", 3)]
    blocks += [halves[1], steps[2], steps[3], swapped(steps[3], "col", 1)]
    pivot_all = lax.all_gather(upper_parent[0], "row", axis=0, tiled=True)
    far_all = lax.all_gather(upper_grand[0], "row", axis=0, tiled=True)
    solve_right, strip = call(
        prepare_kernel,
        [shape((size, size), BF16), shape((size, wide + width), BF16)],
        [
            at, live_width, tile_pattern, pivot_order, *in_hbm(upper_inverse[0], lower_inverse[0]),
            pivot_all, far_all,
        ],
        specs=[SCALARS] * 3 + [pl.BlockSpec(memory_space=pltpu.VMEM)] * 5,
        scratch=[pltpu.VMEM((size, size), BF16)],
        flops=2 * size * size * (size + wide + width),
    )
    panel, right, pivot, below, coded = call(
        lambda *refs: leaf_panel_kernel(rows // TILE, *refs),
        [
            shape((rows, size), BF16),
            shape((height, wide), F32),
            shape((height, width), F32),
            shape((rows, width), F32),
            shape(((wide // TILE + 2) * (height + 16) + rows + 16, width), I16),
        ],
        [
            at, tile_pattern, *blocks, solve_right, strip,
            *in_hbm(parent_block[0], parent_right[0], parent_below[0]),
        ],
        specs=[SCALARS] * 2 + [pl.BlockSpec(memory_space=pltpu.VMEM)] * 13,
        flops=2 * (rows + height) * size * (size + width),
    )

    def leaf_corner(start, count, panel):
        return call(
            leaf_corner_kernel,
            [pltpu.HBM((count, wide), F32), shape((count + 16, wide), I16)],
            [panel, strip, *in_hbm(grand_block[0])],
            specs=[
                pl.BlockSpec((pl.Element(count), pl.Element(size)), lambda j: (start, 0)),
                pl.BlockSpec((size, COLUMNS), lambda j: (0, j)),
                pl.BlockSpec((pl.Element(count), pl.Element(COLUMNS)), lambda j: (start, j * COLUMNS)),
            ],
            grid=(strips,),
            out_specs=[
                pl.BlockSpec((count, COLUMNS), lambda j: (0, j)),
                pl.BlockSpec((count + 16, COLUMNS), lambda j: (0, j)),
            ],
            flops=2 * count * size * wide,
        )

    corner_0, coded_0 = leaf_corner(0, cut, panel)
    corner_1, coded_1 = leaf_corner(cut, rows - cut, panel)

    right, _ = lax.optimization_barrier((right, coded_1))
    coded = swapped(coded, "depth", 1)
    both_mine, below_mine, pivot_pair = call(
        leaf_pair_kernel,
        [shape((2 * rows, width), BF16), shape((rows, width), BF16), shape((height, width), F32)],
        [right, pivot, below, coded],
    )
    both_other = swapped(both_mine, "depth", 3)
    below_other = both_other[:rows]

    def corner_pair(corner, coded):
        count = corner.shape[0]
        specs = [
            pl.BlockSpec((count, COLUMNS), lambda j: (0, j)),
            pl.BlockSpec((count + 16, COLUMNS), lambda j: (0, j)),
        ]
        return call(
            corner_pair_kernel,
            [pltpu.HBM((count, wide), F32), shape((count + 16, wide), I16)],
            [corner, coded],
            specs=specs,
            grid=(strips,),
            out_specs=specs,
        )

    came_0 = swapped(coded_0, "depth", 3)
    came_1 = swapped(coded_1, "depth", 1)
    pair_0, coded_0 = corner_pair(corner_0, came_0)
    pair_1, coded_1 = corner_pair(corner_1, came_1)
    came_0 = swapped(coded_0, "depth", 1)
    came_1 = swapped(coded_1, "depth", 3)

    first = row_index == 0

    def in_row_order(own, traded):
        return jnp.concatenate([jnp.where(first, own, traded), jnp.where(first, traded, own)], axis=0)

    pivots = [pivot_pair, *ring_gather(pivot_pair, "col")]
    inverse_mine, inverse_half = call(
        newton_kernel,
        [shape((size, size), BF16), shape((height, size), BF16)],
        [at, *pivots, swapped(jnp.concatenate(pivots, axis=0), "row", 1)],
        specs=[SCALARS] + [pl.BlockSpec(memory_space=pltpu.VMEM)] * 5,
        scratch=[pltpu.VMEM((size, size), F32), pltpu.VMEM((size, size), F32)],
        flops=2 * 24 * size**3,
    )
    inverse_half = swapped(inverse_half, "depth", 3)
    inverse_other = in_row_order(inverse_half, swapped(inverse_half, "row", 1))

    def level_lower(block, inverse):
        spec = pl.BlockSpec((rows // 2, width), lambda i: (i, 0))
        whole = pl.BlockSpec((size, size), lambda i: (0, 0))
        return call(
            level_lower_kernel,
            [shape((rows, size), BF16)],
            [at, block, *ring_gather(block, "col"), inverse],
            specs=[SCALARS] + [spec] * 4 + [whole],
            grid=(2,),
            out_specs=[pl.BlockSpec((rows // 2, size), lambda i: (i, 0))],
            scratch=[pltpu.VMEM((size, size), BF16)],
            flops=2 * rows * size * size,
        )[0]

    lower_mine = level_lower(below_mine, inverse_mine)
    lower_other = level_lower(below_other, inverse_other)
    right_across = swapped(jnp.concatenate([both_mine[rows:], both_other[rows:]], axis=0), "row", 1)
    (right_all,) = call(
        right_kernel,
        [shape((2 * size, wide), BF16)],
        [at, both_mine, both_other, right_across],
        specs=[SCALARS] + [pl.BlockSpec(memory_space=pltpu.VMEM)] * 3,
    )
    strip_spec = lambda dims: pl.BlockSpec(dims, lambda j: (0, j))
    (update,) = call(
        update_kernel,
        [shape((rows, wide), F32)],
        [pair_0, pair_1, lower_mine, lower_other, right_all],
        specs=[
            strip_spec((cut, COLUMNS)),
            strip_spec((rows - cut, COLUMNS)),
            pl.BlockSpec((rows, size), lambda j: (0, 0)),
            pl.BlockSpec((rows, size), lambda j: (0, 0)),
            strip_spec((2 * size, COLUMNS)),
        ],
        grid=(strips,),
        out_specs=[strip_spec((rows, COLUMNS))],
        flops=4 * rows * size * wide,
    )
    (result,) = call(
        final_kernel,
        [shape((rows, wide), F32)],
        [update, came_0, came_1],
        specs=[
            strip_spec((rows, COLUMNS)),
            strip_spec((cut + 16, COLUMNS)),
            strip_spec((rows - cut + 16, COLUMNS)),
        ],
        grid=(strips,),
        out_specs=[strip_spec((rows, COLUMNS))],
    )
    return result[None]


def solution(mesh):
    return jax.shard_map(
        body,
        mesh=mesh,
        in_specs=(
            P("depth", "row", "col"),
            P("depth", "row", "col"),
            P("depth", "row", "col"),
            P("depth", "row", "col"),
            P("depth", "row", "col"),
            P("depth", "row", "col"),
            P("depth", "row", "col"),
            P("depth", "row", "col"),
            P("depth", None, None),
            P("depth", None, None),
            P("depth", None),
            P("depth"),
            P("depth", None),
        ),
        out_specs=P("depth", "row", "col"),
        check_vma=False,
    )
```

```python
import math

import jax
import jax.numpy as jnp
from jax import lax
from jax.experimental import pallas as pl
from jax.experimental.pallas import tpu as pltpu
from jax.sharding import PartitionSpec as P

TILE = 128
NEWTON = 3
COLUMNS = 256
VMEM = 32 * 2**20
RING = (0, 1, 3, 2)
F32 = jnp.float32
BF16 = jnp.bfloat16
I16 = jnp.int16
SCALARS = pl.BlockSpec(memory_space=pltpu.SMEM)


def swapped(block, axis, mask):
    route = [(low, low ^ mask) for low in range(lax.axis_size(axis))]
    return lax.ppermute(block, axis, route)


def after(value, *others):
    return lax.optimization_barrier((value, *others))[0]


def ring_gather(block, axis):
    return [swapped(block, axis, mask) for mask in RING[1:]]


def dot(left, right):
    return jnp.dot(left, right, preferred_element_type=F32)


def in_hbm(*arrays):
    return [pltpu.with_memory_space_constraint(array, pltpu.HBM) for array in arrays]


def call(kernel, outs, args, specs=None, grid=None, out_specs=None, scratch=(), flops=0, aliases=None, ahead=0):
    size = sum(math.prod(a.shape) * jnp.dtype(a.dtype).itemsize for a in list(args) + list(outs))
    more = {}
    if ahead:
        more["grid_spec"] = pltpu.PrefetchScalarGridSpec(
            num_scalar_prefetch=ahead, grid=grid, in_specs=specs, out_specs=out_specs, scratch_shapes=list(scratch)
        )
    else:
        more["scratch_shapes"] = list(scratch)
        if grid is not None:
            more.update(grid=grid, out_specs=out_specs)
        if specs is not None:
            more["in_specs"] = specs
    if aliases is not None:
        more["input_output_aliases"] = aliases
    return pl.pallas_call(
        kernel,
        out_shape=list(outs),
        compiler_params=pltpu.CompilerParams(vmem_limit_bytes=VMEM),
        cost_estimate=pl.CostEstimate(
            flops=flops, bytes_accessed=size, transcendentals=0
        ),
        **more,
    )(*args)


def shape(dims, dtype):
    return jax.ShapeDtypeStruct(dims, dtype)


def start_at(block, size):
    return pl.ds(pl.multiple_of(block * size, size), size)


def iota(dims, axis):
    return lax.broadcasted_iota(jnp.int32, dims, axis)


def encode(block, coded_ref):
    rows = block.shape[0]
    most = jnp.maximum(jnp.max(jnp.abs(block), axis=0, keepdims=True), 1e-30)
    power = jnp.ceil(jnp.log2(most) + 0.01)
    scale = 0.98 * jnp.exp2(15.0 - power)
    coded_ref[:rows, :] = jnp.round(block * scale).astype(jnp.int32).astype(I16)
    coded_ref[rows:, :] = jnp.broadcast_to(power, (16, block.shape[1])).astype(jnp.int32).astype(I16)


def decode(coded_ref):
    rows = coded_ref.shape[0] - 16
    power = coded_ref[rows:, :].astype(jnp.int32).astype(F32)[:1, :]
    scale = jnp.exp2(power - 15.0) * (1.0 / 0.98)
    return coded_ref[:rows, :].astype(jnp.int32).astype(F32) * scale


def prepare_kernel(
    at, live, tiles, order, upper_inverse, lower_inverse, pivot_all, far_all, solve_right, strip, solve_left,
):
    col = at[1]
    size = upper_inverse.shape[0]
    width = size // len(RING)
    wide = far_all.shape[1]
    shown = iota((width, size), 1) < live[0]
    for k, mask in enumerate(RING):
        block = upper_inverse[start_at(col ^ mask, width), :].astype(F32)
        solve_right[k * width : (k + 1) * width, :] = jnp.where(shown, block, 0.0).astype(BF16)
    chosen = jnp.where(iota((size, size), 0) == order[...], 1.0, 0.0).astype(BF16)
    masked = jnp.where(iota((size, size), 0) < live[0], lower_inverse[...].astype(F32), 0.0).astype(BF16)
    solve_left[...] = lax.dot_general(
        masked, chosen, (((1,), (1,)), ((), ())), preferred_element_type=F32
    ).astype(BF16)
    count = wide // TILE
    far = dot(solve_left[...], far_all[...])
    for t in range(count):
        flag = tiles[0, col * count + t].astype(F32)
        strip[:, t * TILE : (t + 1) * TILE] = (far[:, t * TILE : (t + 1) * TILE] * flag).astype(BF16)
    strip[:, wide:] = dot(solve_left[...], pivot_all[...]).astype(BF16)


def leaf_panel_kernel(tile_count, at, tiles, *refs):
    blocks, (solve_right, strip, parent_block, parent_right, parent_below) = refs[:8], refs[8:13]
    panel, right, pivot, below, coded = refs[13:]
    row = at[0]
    height, wide = parent_right.shape
    rows = parent_below.shape[0]
    cut = blocks[0].shape[0]
    for part in (0, 1):
        lower = jnp.concatenate([ref[...] for ref in blocks[4 * part : 4 * part + 4]], axis=1)
        whole = dot(lower, solve_right[...])
        for t in range((rows - cut if part else cut) // TILE):
            flag = tiles[0, row * tile_count + part * (cut // TILE) + t].astype(F32)
            panel[part * cut + t * TILE : part * cut + (t + 1) * TILE, :] = (
                whole[t * TILE : (t + 1) * TILE, :] * flag
            ).astype(BF16)
    parent = whole[rows - cut :, :].astype(BF16)
    here = 0
    found = parent_right[...] - dot(parent, strip[:, :wide])
    right[...] = found
    for k in range(wide // TILE):
        encode(found[:, k * TILE : (k + 1) * TILE], coded.at[here : here + height + 16, :])
        here += height + 16
    found = parent_block[...] - dot(parent, strip[:, wide:])
    pivot[...] = found
    found = parent_below[...] - dot(panel[...], strip[:, wide:])
    below[...] = found
    encode(found, coded.at[here:, :])


def leaf_pair_kernel(right, below, coded, both, below_pair):
    height, wide = right.shape
    rows = below.shape[0]
    here = 0
    for k in range(wide // TILE):
        came = decode(coded.at[here : here + height + 16, :])
        both[rows + k * height : rows + (k + 1) * height, :] = (
            right[:, k * TILE : (k + 1) * TILE] + came
        ).astype(BF16)
        here += height + 16
    total = (below[...] + decode(coded.at[here:, :])).astype(BF16)
    below_pair[...] = total
    both[:rows, :] = total


def split_kernel(mine, other, below_other, rights):
    rows = mine.shape[0] // 2
    below_other[...] = other[:rows, :]
    rights[:rows, :] = mine[rows:, :]
    rights[rows:, :] = other[rows:, :]


def corner_give_kernel(at, panel, far, grand, coded):
    encode(grand[...] - dot(panel[...], far[...]), coded)


def corner_pair_kernel(at, panel, far, grand, came, total, coded):
    block = grand[...] - dot(panel[...], far[...]) + decode(came)
    total[...] = block
    encode(block, coded)


def corner_quad_kernel(pair, came, total, coded):
    block = pair[...] + decode(came)
    total[...] = block
    encode(block, coded)


def parts_of(block):
    high = block.astype(BF16)
    return high, (block - high.astype(F32)).astype(BF16)


def dot_wide(left, right):
    left_high, left_low = left
    right_high, right_low = right
    return dot(left_high, right_high) + (dot(left_high, right_low) + dot(left_low, right_high))


def newton_kernel(at, block_0, block_1, block_3, block_2, across, out, half, matrix, inverse):
    row, col = at[0], at[1]
    size = matrix.shape[0]
    height, width = block_0.shape
    for k, (mask, block) in enumerate(zip(RING, (block_0, block_1, block_3, block_2))):
        matrix[start_at(row, height), start_at(col ^ mask, width)] = block[...]
        matrix[start_at(1 - row, height), start_at(col ^ mask, width)] = across[k * height : (k + 1) * height, :]
    where = iota((size, size), 0) == iota((size, size), 1)
    only = jnp.where(where, matrix[...], 0.0)
    by_row = 1.0 / jnp.sum(only, axis=1, keepdims=True)
    by_col = 1.0 / jnp.sum(only, axis=0, keepdims=True)
    inverse[...] = jnp.where(where, 2.0 * by_col, 0.0) - by_row * (matrix[...] * by_col)
    whole = parts_of(matrix[...])
    for step in range(NEWTON - 1):
        held = parts_of(inverse[...])
        inverse[...] = 2.0 * inverse[...] - dot_wide(held, parts_of(dot_wide(whole, held)))
    out[...] = inverse[...].astype(BF16)
    half[...] = inverse[start_at(row, half.shape[0]), :].astype(BF16)


def lower_kernel(at, own, near, far, across_0, across_1, *rest):
    *inverses, out, ordered, whole = rest
    row, col = at[0], at[1]
    size = ordered.shape[0]

    @pl.when(pl.program_id(0) == 0)
    def _():
        if len(inverses) == 1:
            whole[...] = inverses[0][...]
        else:
            whole[start_at(row, size // 2), :] = inverses[0][...]
            whole[start_at(1 - row, size // 2), :] = inverses[1][...]
        for k, mask in enumerate(RING):
            ordered[k * TILE : (k + 1) * TILE, :] = whole[start_at(col ^ mask, TILE), :]

    for part, across in ((0, across_0), (1, across_1)):

        @pl.when(pl.program_id(0) == part)
        def _():
            lower = jnp.concatenate([own[...], near[...], far[...], across[...]], axis=1)
            out[...] = dot(lower, ordered[...]).astype(BF16)


def halves_kernel(near, far, first, second):
    rows = first.shape[0]
    first[...] = near[:rows, :]
    second[...] = far[rows:, :]


def right_kernel(at, rights, across, out):
    row = at[0]
    count = out.shape[1] // TILE
    height = rights.shape[0] // (2 * count)
    for pair in (0, 1):
        for k in range(count):
            strip = slice(k * TILE, (k + 1) * TILE)
            here = slice((pair * count + k) * height, (pair * count + k + 1) * height)
            out[start_at(2 * pair + row, height), strip] = rights[here, :]
            out[start_at(2 * pair + 1 - row, height), strip] = across[here, :]


def final_kernel(at, own_0, came_0, own_1, came_1, lower_mine, lower_other, right, out):
    size = lower_mine.shape[1]
    update = dot(lower_mine[...], right[:size, :]) + dot(lower_other[...], right[size:, :])
    for k, ref in enumerate((own_0, came_0, own_1, came_1)):

        @pl.when(pl.program_id(0) == k)
        def _():
            out[...] = (decode(ref) if k % 2 else ref[...]) - update


def body(
    parent_block,
    parent_right,
    parent_below,
    grand_block,
    lower_parent,
    lower_grand,
    upper_parent,
    upper_grand,
    lower_inverse,
    upper_inverse,
    pivot_order,
    live_width,
    tile_pattern,
):
    row_index = lax.axis_index("row")
    col_index = lax.axis_index("col")
    depth_index = lax.axis_index("depth")
    h = (depth_index >> 1) & 1
    g = (depth_index ^ (depth_index >> 1)) & 1
    at = jnp.stack([row_index, col_index, g, h])
    size = upper_inverse.shape[2]
    rows, wide = grand_block.shape[1:]
    width = lower_grand.shape[2]
    strips = wide // COLUMNS

    height = parent_right.shape[1]
    cut = (rows + height) // 2
    halves = [lower_grand[0][:cut], jnp.concatenate([lower_grand[0][cut:], lower_parent[0]], axis=0)]
    steps = [swapped(half, "col", mask) for half in halves for mask in (1, 3)]
    blocks = [halves[0], steps[0], steps[1], swapped(steps[0], "col", 3)]
    blocks += [halves[1], steps[2], steps[3], swapped(steps[3], "col", 1)]
    pivot_all = lax.all_gather(upper_parent[0], "row", axis=0, tiled=True)
    far_all = lax.all_gather(upper_grand[0], "row", axis=0, tiled=True)
    solve_right, strip = call(
        prepare_kernel,
        [shape((size, size), BF16), shape((size, wide + width), BF16)],
        [
            at, live_width, tile_pattern, pivot_order, *in_hbm(upper_inverse[0], lower_inverse[0]),
            pivot_all, far_all,
        ],
        specs=[SCALARS] * 3 + [pl.BlockSpec(memory_space=pltpu.VMEM)] * 5,
        scratch=[pltpu.VMEM((size, size), BF16)],
        flops=2 * size * size * (size + wide + width),
    )
    panel, right, pivot, below, coded = call(
        lambda *refs: leaf_panel_kernel(rows // TILE, *refs),
        [
            shape((rows, size), BF16),
            shape((height, wide), F32),
            shape((height, width), F32),
            shape((rows, width), F32),
            shape((wide // TILE * (height + 16) + rows + 16, width), I16),
        ],
        [
            at, tile_pattern, *blocks, solve_right, strip,
            *in_hbm(parent_block[0], parent_right[0], parent_below[0]),
        ],
        specs=[SCALARS] * 2 + [pl.BlockSpec(memory_space=pltpu.VMEM)] * 13,
        flops=2 * (rows + height) * size * (size + width),
    )

    half = rows // 4
    coded_spec = pl.BlockSpec((half + 16, COLUMNS), lambda j, at: (0, j))
    total_spec = pl.BlockSpec((half, COLUMNS), lambda j, at: (0, j))

    def corner(kernel, place, came, panel):
        return call(
            kernel,
            [shape((half, wide), F32)] * len(came) + [shape((half + 16, wide), I16)],
            [at, panel, strip, *in_hbm(grand_block[0]), *came],
            specs=[
                pl.BlockSpec((half, size), lambda j, at: (place(at), 0)),
                pl.BlockSpec((size, COLUMNS), lambda j, at: (0, j)),
                pl.BlockSpec((half, COLUMNS), lambda j, at: (place(at), j)),
            ]
            + [coded_spec] * len(came),
            grid=(strips,),
            out_specs=[total_spec] * len(came) + [coded_spec],
            flops=2 * half * size * wide,
            ahead=1,
        )

    def corner_quad(pair, came):
        specs = [pl.BlockSpec((half, COLUMNS), lambda j: (0, j)), pl.BlockSpec((half + 16, COLUMNS), lambda j: (0, j))]
        return call(
            corner_quad_kernel,
            [shape((half, wide), F32), shape((half + 16, wide), I16)],
            [pair, came],
            specs=specs,
            grid=(strips,),
            out_specs=specs,
        )

    (give_1,) = corner(corner_give_kernel, lambda at: 3 - at[3], [], panel)
    (give_0,) = corner(corner_give_kernel, lambda at: 1 - at[2], [], after(panel, give_1))
    step_1 = swapped(give_1, "depth", 3)
    step_0 = swapped(give_0, "depth", 1)

    pivot_pair = pivot + after(swapped(pivot, "depth", 1), give_0)
    pivots = [pivot_pair, *ring_gather(pivot_pair, "col")]
    pivots_across = swapped(jnp.concatenate(pivots, axis=0), "row", 1)

    both_mine, below_mine = call(
        leaf_pair_kernel,
        [shape((2 * rows, width), BF16), shape((rows, width), BF16)],
        [after(right, step_1, pivots_across), below, swapped(coded, "depth", 1)],
    )
    both_other = swapped(both_mine, "depth", 3)

    def near_blocks(block):
        return swapped(block, "col", 1), swapped(block, "col", 3)

    def across_blocks(near, far):
        piece = shape((rows // 2, width), BF16)
        first, second = call(halves_kernel, [piece, piece], [near, far])
        return first, [swapped(first, "col", 3), swapped(second, "col", 1)]

    near_mine = near_blocks(below_mine)
    inverse_mine, inverse_half = call(
        newton_kernel,
        [shape((size, size), BF16), shape((height, size), BF16)],
        [at, *pivots, after(pivots_across, below_mine)],
        specs=[SCALARS] + [pl.BlockSpec(memory_space=pltpu.VMEM)] * 5,
        scratch=[pltpu.VMEM((size, size), F32), pltpu.VMEM((size, size), F32)],
        flops=2 * 12 * size**3,
    )
    inverse_half = swapped(inverse_half, "depth", 3)
    pair_1, coded_1 = corner(
        corner_pair_kernel, lambda at: 2 + at[3], [step_1], after(panel, inverse_mine)
    )
    came_1 = swapped(coded_1, "depth", 1)
    sent_mine, across_mine = across_blocks(near_mine[0], after(near_mine[1], coded_1))
    pair_0, coded_0 = corner(
        corner_pair_kernel, lambda at: at[2], [step_0], after(panel, sent_mine)
    )
    came_0 = swapped(coded_0, "depth", 3)

    def level_lower(block, near, across, inverses):
        block_spec = pl.BlockSpec((rows // 2, width), lambda i: (i, 0))
        across_spec = pl.BlockSpec((rows // 2, width), lambda i: (0, 0))
        return call(
            lower_kernel,
            [shape((rows, size), BF16)],
            [at, block, *near, *across, *inverses],
            specs=[SCALARS]
            + [block_spec] * 3
            + [across_spec] * 2
            + [pl.BlockSpec(one.shape, lambda i: (0, 0)) for one in inverses],
            grid=(2,),
            out_specs=[pl.BlockSpec((rows // 2, size), lambda i: (i, 0))],
            scratch=[pltpu.VMEM((size, size), BF16)] * 2,
            flops=2 * rows * size * size,
        )[0]

    lower_mine = level_lower(below_mine, near_mine, across_mine, [after(inverse_mine, coded_0)])
    below_other, rights = call(
        split_kernel,
        [shape((rows, width), BF16), shape((2 * rows, width), BF16)],
        [both_mine, after(both_other, inverse_half, lower_mine)],
    )
    near_other = near_blocks(below_other)
    inverse_across = swapped(after(inverse_half, rights), "row", 1)
    own_1, coded_1 = corner_quad(after(pair_1, rights), came_1)
    came_1 = swapped(coded_1, "depth", 3)
    sent_other, across_other = across_blocks(near_other[0], after(near_other[1], coded_1, inverse_across))
    own_0, coded_0 = corner_quad(after(pair_0, sent_other), came_0)
    came_0 = swapped(coded_0, "depth", 1)
    (right_all,) = call(
        right_kernel,
        [shape((2 * size, wide), BF16)],
        [at, rights, after(swapped(rights, "row", 1), coded_0)],
        specs=[SCALARS] + [pl.BlockSpec(memory_space=pltpu.VMEM)] * 2,
    )
    lower_other = level_lower(
        below_other, near_other, across_other, [inverse_half, after(inverse_across, right_all)]
    )

    place = lambda k, at: jnp.where(k == 0, at[2], jnp.where(k == 1, 1 - at[2], jnp.where(k == 2, 2 + at[3], 3 - at[3])))
    own_spec = pl.BlockSpec((half, wide), lambda k, at: (0, 0))
    came_spec = pl.BlockSpec((half + 16, wide), lambda k, at: (0, 0))
    lower_spec = pl.BlockSpec((half, size), lambda k, at: (place(k, at), 0))
    (result,) = call(
        final_kernel,
        [shape((rows, wide), F32)],
        [at, own_0, came_0, own_1, came_1, lower_mine, lower_other, right_all],
        specs=[own_spec, came_spec] * 2
        + [lower_spec] * 2
        + [pl.BlockSpec((2 * size, wide), lambda k, at: (0, 0))],
        grid=(4,),
        out_specs=[pl.BlockSpec((half, wide), lambda k, at: (place(k, at), 0))],
        flops=4 * rows * size * wide,
        ahead=1,
    )
    return result[None]


def solution(mesh):
    return jax.shard_map(
        body,
        mesh=mesh,
        in_specs=(
            P("depth", "row", "col"),
            P("depth", "row", "col"),
            P("depth", "row", "col"),
            P("depth", "row", "col"),
            P("depth", "row", "col"),
            P("depth", "row", "col"),
            P("depth", "row", "col"),
            P("depth", "row", "col"),
            P("depth", None, None),
            P("depth", None, None),
            P("depth", None),
            P("depth"),
            P("depth", None),
        ),
        out_specs=P("depth", "row", "col"),
        check_vma=False,
    )
```

```python
import math

import jax
import jax.numpy as jnp
from jax import lax
from jax.experimental import pallas as pl
from jax.experimental.pallas import tpu as pltpu
from jax.sharding import PartitionSpec as P

TILE = 128
NEWTON = 3
COLUMNS = 256
VMEM = 32 * 2**20
RING = (0, 1, 3, 2)
F32 = jnp.float32
BF16 = jnp.bfloat16
I16 = jnp.int16
SCALARS = pl.BlockSpec(memory_space=pltpu.SMEM)


def swapped(block, axis, mask):
    route = [(low, low ^ mask) for low in range(lax.axis_size(axis))]
    return lax.ppermute(block, axis, route)


def after(value, *others):
    return lax.optimization_barrier((value, *others))[0]


def ring_gather(block, axis):
    return [swapped(block, axis, mask) for mask in RING[1:]]


def dot(left, right):
    return jnp.dot(left, right, preferred_element_type=F32)


def in_hbm(*arrays):
    return [pltpu.with_memory_space_constraint(array, pltpu.HBM) for array in arrays]


def call(kernel, outs, args, specs=None, grid=None, out_specs=None, scratch=(), flops=0, aliases=None, ahead=0):
    size = sum(math.prod(a.shape) * jnp.dtype(a.dtype).itemsize for a in list(args) + list(outs))
    more = {}
    if ahead:
        more["grid_spec"] = pltpu.PrefetchScalarGridSpec(
            num_scalar_prefetch=ahead, grid=grid, in_specs=specs, out_specs=out_specs, scratch_shapes=list(scratch)
        )
    else:
        more["scratch_shapes"] = list(scratch)
        if grid is not None:
            more.update(grid=grid, out_specs=out_specs)
        if specs is not None:
            more["in_specs"] = specs
    if aliases is not None:
        more["input_output_aliases"] = aliases
    return pl.pallas_call(
        kernel,
        out_shape=list(outs),
        compiler_params=pltpu.CompilerParams(vmem_limit_bytes=VMEM),
        cost_estimate=pl.CostEstimate(
            flops=flops, bytes_accessed=size, transcendentals=0
        ),
        **more,
    )(*args)


def shape(dims, dtype):
    return jax.ShapeDtypeStruct(dims, dtype)


def start_at(block, size):
    return pl.ds(pl.multiple_of(block * size, size), size)


def iota(dims, axis):
    return lax.broadcasted_iota(jnp.int32, dims, axis)


def encode(block, coded_ref):
    rows = block.shape[0]
    most = jnp.maximum(jnp.max(jnp.abs(block), axis=0, keepdims=True), 1e-30)
    power = jnp.ceil(jnp.log2(most) + 0.01)
    scale = 0.98 * jnp.exp2(15.0 - power)
    coded_ref[:rows, :] = jnp.round(block * scale).astype(jnp.int32).astype(I16)
    coded_ref[rows:, :] = jnp.broadcast_to(power, (16, block.shape[1])).astype(jnp.int32).astype(I16)


def decode(coded_ref):
    rows = coded_ref.shape[0] - 16
    power = coded_ref[rows:, :].astype(jnp.int32).astype(F32)[:1, :]
    scale = jnp.exp2(power - 15.0) * (1.0 / 0.98)
    return coded_ref[:rows, :].astype(jnp.int32).astype(F32) * scale


def prepare_kernel(
    at, live, tiles, order, upper_inverse, lower_inverse, pivot_all, far_all, solve_right, strip, solve_left,
):
    col = at[1]
    size = upper_inverse.shape[0]
    width = size // len(RING)
    wide = far_all.shape[1]
    shown = iota((width, size), 1) < live[0]
    for k, mask in enumerate(RING):
        block = upper_inverse[start_at(col ^ mask, width), :].astype(F32)
        solve_right[k * width : (k + 1) * width, :] = jnp.where(shown, block, 0.0).astype(BF16)
    chosen = jnp.where(iota((size, size), 0) == order[...], 1.0, 0.0).astype(BF16)
    masked = jnp.where(iota((size, size), 0) < live[0], lower_inverse[...].astype(F32), 0.0).astype(BF16)
    solve_left[...] = lax.dot_general(
        masked, chosen, (((1,), (1,)), ((), ())), preferred_element_type=F32
    ).astype(BF16)
    count = wide // TILE
    far = dot(solve_left[...], far_all[...])
    for t in range(count):
        flag = tiles[0, col * count + t].astype(F32)
        strip[:, t * TILE : (t + 1) * TILE] = (far[:, t * TILE : (t + 1) * TILE] * flag).astype(BF16)
    strip[:, wide:] = dot(solve_left[...], pivot_all[...]).astype(BF16)


def leaf_panel_kernel(tile_count, at, tiles, *refs):
    blocks, (solve_right, strip, parent_block, parent_right, parent_below) = refs[:8], refs[8:13]
    panel, right, pivot, below, coded = refs[13:]
    row = at[0]
    height, wide = parent_right.shape
    rows = parent_below.shape[0]
    cut = blocks[0].shape[0]
    for part in (0, 1):
        lower = jnp.concatenate([ref[...] for ref in blocks[4 * part : 4 * part + 4]], axis=1)
        whole = dot(lower, solve_right[...])
        for t in range((rows - cut if part else cut) // TILE):
            flag = tiles[0, row * tile_count + part * (cut // TILE) + t].astype(F32)
            panel[part * cut + t * TILE : part * cut + (t + 1) * TILE, :] = (
                whole[t * TILE : (t + 1) * TILE, :] * flag
            ).astype(BF16)
    parent = whole[rows - cut :, :].astype(BF16)
    here = 0
    found = parent_right[...] - dot(parent, strip[:, :wide])
    right[...] = found
    for k in range(wide // TILE):
        encode(found[:, k * TILE : (k + 1) * TILE], coded.at[here : here + height + 16, :])
        here += height + 16
    found = parent_block[...] - dot(parent, strip[:, wide:])
    pivot[...] = found
    found = parent_below[...] - dot(panel[...], strip[:, wide:])
    below[...] = found
    encode(found, coded.at[here:, :])


def leaf_pair_kernel(right, below, coded, both, below_pair):
    height, wide = right.shape
    rows = below.shape[0]
    here = 0
    for k in range(wide // TILE):
        came = decode(coded.at[here : here + height + 16, :])
        both[rows + k * height : rows + (k + 1) * height, :] = (
            right[:, k * TILE : (k + 1) * TILE] + came
        ).astype(BF16)
        here += height + 16
    total = (below[...] + decode(coded.at[here:, :])).astype(BF16)
    below_pair[...] = total
    both[:rows, :] = total


def split_kernel(mine, other, below_other, rights):
    rows = mine.shape[0] // 2
    below_other[...] = other[:rows, :]
    rights[:rows, :] = mine[rows:, :]
    rights[rows:, :] = other[rows:, :]


def corner_give_kernel(at, panel, far, grand, coded):
    encode(grand[...] - dot(panel[...], far[...]), coded)


def corner_pair_kernel(at, panel, far, grand, came, total, coded):
    block = grand[...] - dot(panel[...], far[...]) + decode(came)
    total[...] = block
    encode(block, coded)


def corner_quad_kernel(pair, came, total, coded):
    block = pair[...] + decode(came)
    total[...] = block
    encode(block, coded)


def parts_of(block):
    high = block.astype(BF16)
    return high, (block - high.astype(F32)).astype(BF16)


def dot_wide(left, right):
    left_high, left_low = left
    right_high, right_low = right
    return dot(left_high, right_high) + (dot(left_high, right_low) + dot(left_low, right_high))


def newton_kernel(at, block_0, block_1, block_3, block_2, across, out, half, matrix, inverse):
    row, col = at[0], at[1]
    size = matrix.shape[0]
    height, width = block_0.shape
    for k, (mask, block) in enumerate(zip(RING, (block_0, block_1, block_3, block_2))):
        matrix[start_at(row, height), start_at(col ^ mask, width)] = block[...]
        matrix[start_at(1 - row, height), start_at(col ^ mask, width)] = across[k * height : (k + 1) * height, :]
    where = iota((size, size), 0) == iota((size, size), 1)
    only = jnp.where(where, matrix[...], 0.0)
    by_row = 1.0 / jnp.sum(only, axis=1, keepdims=True)
    by_col = 1.0 / jnp.sum(only, axis=0, keepdims=True)
    inverse[...] = jnp.where(where, 2.0 * by_col, 0.0) - by_row * (matrix[...] * by_col)
    whole = parts_of(matrix[...])
    for step in range(NEWTON - 1):
        held = parts_of(inverse[...])
        inverse[...] = 2.0 * inverse[...] - dot_wide(held, parts_of(dot_wide(whole, held)))
    out[...] = inverse[...].astype(BF16)
    half[...] = inverse[start_at(row, half.shape[0]), :].astype(BF16)


def lower_kernel(at, own, near, far, across_0, across_1, *rest):
    *inverses, out, ordered, whole = rest
    row, col = at[0], at[1]
    size = ordered.shape[0]

    @pl.when(pl.program_id(0) == 0)
    def _():
        if len(inverses) == 1:
            whole[...] = inverses[0][...]
        else:
            whole[start_at(row, size // 2), :] = inverses[0][...]
            whole[start_at(1 - row, size // 2), :] = inverses[1][...]
        for k, mask in enumerate(RING):
            ordered[k * TILE : (k + 1) * TILE, :] = whole[start_at(col ^ mask, TILE), :]

    for part, across in ((0, across_0), (1, across_1)):

        @pl.when(pl.program_id(0) == part)
        def _():
            lower = jnp.concatenate([own[...], near[...], far[...], across[...]], axis=1)
            out[...] = dot(lower, ordered[...]).astype(BF16)


def halves_kernel(near, far, first, second):
    rows = first.shape[0]
    first[...] = near[:rows, :]
    second[...] = far[rows:, :]


def right_kernel(at, rights, across, out):
    row = at[0]
    count = out.shape[1] // TILE
    height = rights.shape[0] // (2 * count)
    for pair in (0, 1):
        for k in range(count):
            strip = slice(k * TILE, (k + 1) * TILE)
            here = slice((pair * count + k) * height, (pair * count + k + 1) * height)
            out[start_at(2 * pair + row, height), strip] = rights[here, :]
            out[start_at(2 * pair + 1 - row, height), strip] = across[here, :]


def final_kernel(at, own_0, came_0, own_1, came_1, lower_mine, lower_other, right, out):
    size = lower_mine.shape[1]
    update = dot(lower_mine[...], right[:size, :]) + dot(lower_other[...], right[size:, :])
    for k, ref in enumerate((own_0, came_0, own_1, came_1)):

        @pl.when(pl.program_id(0) == k)
        def _():
            out[...] = (decode(ref) if k % 2 else ref[...]) - update


def body(
    parent_block,
    parent_right,
    parent_below,
    grand_block,
    lower_parent,
    lower_grand,
    upper_parent,
    upper_grand,
    lower_inverse,
    upper_inverse,
    pivot_order,
    live_width,
    tile_pattern,
):
    row_index = lax.axis_index("row")
    col_index = lax.axis_index("col")
    depth_index = lax.axis_index("depth")
    h = (depth_index >> 1) & 1
    g = (depth_index ^ (depth_index >> 1)) & 1
    at = jnp.stack([row_index, col_index, g, h])
    size = upper_inverse.shape[2]
    rows, wide = grand_block.shape[1:]
    width = lower_grand.shape[2]
    strips = wide // COLUMNS

    height = parent_right.shape[1]
    cut = (rows + height) // 2
    halves = [lower_grand[0][:cut], jnp.concatenate([lower_grand[0][cut:], lower_parent[0]], axis=0)]
    steps = [swapped(half, "col", mask) for half in halves for mask in (1, 3)]
    blocks = [halves[0], steps[0], steps[1], swapped(steps[0], "col", 3)]
    blocks += [halves[1], steps[2], steps[3], swapped(steps[3], "col", 1)]
    pivot_all = lax.all_gather(upper_parent[0], "row", axis=0, tiled=True)
    far_all = lax.all_gather(upper_grand[0], "row", axis=0, tiled=True)
    solve_right, strip = call(
        prepare_kernel,
        [shape((size, size), BF16), shape((size, wide + width), BF16)],
        [
            at, live_width, tile_pattern, pivot_order, *in_hbm(upper_inverse[0], lower_inverse[0]),
            pivot_all, far_all,
        ],
        specs=[SCALARS] * 3 + [pl.BlockSpec(memory_space=pltpu.VMEM)] * 5,
        scratch=[pltpu.VMEM((size, size), BF16)],
        flops=2 * size * size * (size + wide + width),
    )
    panel, right, pivot, below, coded = call(
        lambda *refs: leaf_panel_kernel(rows // TILE, *refs),
        [
            shape((rows, size), BF16),
            shape((height, wide), F32),
            shape((height, width), F32),
            shape((rows, width), F32),
            shape((wide // TILE * (height + 16) + rows + 16, width), I16),
        ],
        [
            at, tile_pattern, *blocks, solve_right, strip,
            *in_hbm(parent_block[0], parent_right[0], parent_below[0]),
        ],
        specs=[SCALARS] * 2 + [pl.BlockSpec(memory_space=pltpu.VMEM)] * 13,
        flops=2 * (rows + height) * size * (size + width),
    )

    half = rows // 4
    coded_spec = pl.BlockSpec((half + 16, COLUMNS), lambda j, at: (0, j))
    total_spec = pl.BlockSpec((half, COLUMNS), lambda j, at: (0, j))

    def corner(kernel, place, came, panel):
        return call(
            kernel,
            [shape((half, wide), F32)] * len(came) + [shape((half + 16, wide), I16)],
            [at, panel, strip, *in_hbm(grand_block[0]), *came],
            specs=[
                pl.BlockSpec((half, size), lambda j, at: (place(at), 0)),
                pl.BlockSpec((size, COLUMNS), lambda j, at: (0, j)),
                pl.BlockSpec((half, COLUMNS), lambda j, at: (place(at), j)),
            ]
            + [coded_spec] * len(came),
            grid=(strips,),
            out_specs=[total_spec] * len(came) + [coded_spec],
            flops=2 * half * size * wide,
            ahead=1,
        )

    def corner_quad(pair, came):
        specs = [pl.BlockSpec((half, COLUMNS), lambda j: (0, j)), pl.BlockSpec((half + 16, COLUMNS), lambda j: (0, j))]
        return call(
            corner_quad_kernel,
            [shape((half, wide), F32), shape((half + 16, wide), I16)],
            [pair, came],
            specs=specs,
            grid=(strips,),
            out_specs=specs,
        )

    (give_1,) = corner(corner_give_kernel, lambda at: 3 - at[3], [], panel)
    step_1 = swapped(give_1, "depth", 3)

    pivot_pair = pivot + after(swapped(pivot, "depth", 1), give_1)
    pivots = [pivot_pair, *ring_gather(pivot_pair, "col")]
    (give_0,) = corner(corner_give_kernel, lambda at: 1 - at[2], [], after(panel, pivot_pair))
    step_0 = swapped(give_0, "depth", 1)
    pivots = lax.optimization_barrier((pivots, give_0))[0]
    pivots_across = swapped(jnp.concatenate(pivots, axis=0), "row", 1)

    both_mine, below_mine = call(
        leaf_pair_kernel,
        [shape((2 * rows, width), BF16), shape((rows, width), BF16)],
        [after(right, step_1, pivots_across), below, swapped(coded, "depth", 1)],
    )
    both_other = swapped(both_mine, "depth", 3)

    def near_blocks(block):
        return swapped(block, "col", 1), swapped(block, "col", 3)

    def across_blocks(near, far):
        piece = shape((rows // 2, width), BF16)
        first, second = call(halves_kernel, [piece, piece], [near, far])
        return first, [swapped(first, "col", 3), swapped(second, "col", 1)]

    near_mine = near_blocks(below_mine)
    inverse_mine, inverse_half = call(
        newton_kernel,
        [shape((size, size), BF16), shape((height, size), BF16)],
        [at, *pivots, after(pivots_across, below_mine)],
        specs=[SCALARS] + [pl.BlockSpec(memory_space=pltpu.VMEM)] * 5,
        scratch=[pltpu.VMEM((size, size), F32), pltpu.VMEM((size, size), F32)],
        flops=2 * 12 * size**3,
    )
    inverse_half = swapped(inverse_half, "depth", 3)
    pair_1, coded_1 = corner(
        corner_pair_kernel, lambda at: 2 + at[3], [step_1], after(panel, inverse_mine)
    )
    came_1 = swapped(coded_1, "depth", 1)
    sent_mine, across_mine = across_blocks(near_mine[0], after(near_mine[1], coded_1))
    pair_0, coded_0 = corner(
        corner_pair_kernel, lambda at: at[2], [step_0], after(panel, sent_mine)
    )
    came_0 = swapped(coded_0, "depth", 3)

    def level_lower(block, near, across, inverses):
        block_spec = pl.BlockSpec((rows // 2, width), lambda i: (i, 0))
        across_spec = pl.BlockSpec((rows // 2, width), lambda i: (0, 0))
        return call(
            lower_kernel,
            [shape((rows, size), BF16)],
            [at, block, *near, *across, *inverses],
            specs=[SCALARS]
            + [block_spec] * 3
            + [across_spec] * 2
            + [pl.BlockSpec(one.shape, lambda i: (0, 0)) for one in inverses],
            grid=(2,),
            out_specs=[pl.BlockSpec((rows // 2, size), lambda i: (i, 0))],
            scratch=[pltpu.VMEM((size, size), BF16)] * 2,
            flops=2 * rows * size * size,
        )[0]

    lower_mine = level_lower(below_mine, near_mine, across_mine, [after(inverse_mine, coded_0)])
    below_other, rights = call(
        split_kernel,
        [shape((rows, width), BF16), shape((2 * rows, width), BF16)],
        [both_mine, after(both_other, inverse_half, lower_mine)],
    )
    near_other = near_blocks(below_other)
    inverse_across = swapped(after(inverse_half, rights), "row", 1)
    own_1, coded_1 = corner_quad(after(pair_1, rights), came_1)
    came_1 = swapped(coded_1, "depth", 3)
    sent_other, across_other = across_blocks(near_other[0], after(near_other[1], coded_1, inverse_across))
    own_0, coded_0 = corner_quad(after(pair_0, sent_other), came_0)
    came_0 = swapped(coded_0, "depth", 1)
    (right_all,) = call(
        right_kernel,
        [shape((2 * size, wide), BF16)],
        [at, rights, after(swapped(rights, "row", 1), coded_0)],
        specs=[SCALARS] + [pl.BlockSpec(memory_space=pltpu.VMEM)] * 2,
    )
    lower_other = level_lower(
        below_other, near_other, across_other, [inverse_half, after(inverse_across, right_all)]
    )

    place = lambda k, at: jnp.where(k == 0, at[2], jnp.where(k == 1, 1 - at[2], jnp.where(k == 2, 2 + at[3], 3 - at[3])))
    own_spec = pl.BlockSpec((half, wide), lambda k, at: (0, 0))
    came_spec = pl.BlockSpec((half + 16, wide), lambda k, at: (0, 0))
    lower_spec = pl.BlockSpec((half, size), lambda k, at: (place(k, at), 0))
    (result,) = call(
        final_kernel,
        [shape((rows, wide), F32)],
        [at, own_0, came_0, own_1, came_1, lower_mine, lower_other, right_all],
        specs=[own_spec, came_spec] * 2
        + [lower_spec] * 2
        + [pl.BlockSpec((2 * size, wide), lambda k, at: (0, 0))],
        grid=(4,),
        out_specs=[pl.BlockSpec((half, wide), lambda k, at: (place(k, at), 0))],
        flops=4 * rows * size * wide,
        ahead=1,
    )
    return result[None]


def solution(mesh):
    return jax.shard_map(
        body,
        mesh=mesh,
        in_specs=(
            P("depth", "row", "col"),
            P("depth", "row", "col"),
            P("depth", "row", "col"),
            P("depth", "row", "col"),
            P("depth", "row", "col"),
            P("depth", "row", "col"),
            P("depth", "row", "col"),
            P("depth", "row", "col"),
            P("depth", None, None),
            P("depth", None, None),
            P("depth", None),
            P("depth"),
            P("depth", None),
        ),
        out_specs=P("depth", "row", "col"),
        check_vma=False,
    )
```
